32 devices in a mesh: slab: 8 (over z, y), cross: 4 (over x, core).
Axes of the slice: x: 2, y: 2, z: 4, core: 2. Of those that a mesh axis runs over, the one named last changes fastest.
Arguments:
- state: float32 [5, 16, 4096], P(None, 'slab', 'cross'), may hold values from -1.2 to 1.2
- rhs: float32 [5, 16, 4096], P(None, 'slab', 'cross'), may hold values from -1.2 to 1.2
- dinv: float32 [5, 5, 16, 4096], P(None, None, 'slab', 'cross'), may hold values from -0.3 to 2.3, as said below
- lower_jac: float32 [5, 5, 16, 4096], P(None, None, 'slab', 'cross'), may hold values from -0.3 to 2.3
- upper_jac: float32 [5, 5, 16, 4096], P(None, None, 'slab', 'cross'), may hold values from -0.3 to 2.3
- owner: int32 [32768, 1], P(('slab', 'cross')), may hold values from 0 to 31; in each aligned block of 1024 rows (0 to 1023, 1024 to 2047, ...) at most 128 rows name the same one
- donor_block: int32 [32768], P(('slab', 'cross')), may hold values from 0 to 15
- offsets: int32 [8, 32768], P(None, ('slab', 'cross')), may hold values from 0 to 127
- weights: float32 [8, 32768], P(None, ('slab', 'cross')), may hold values from 0 to 1, as said below
- receptor_perm: int32 [32, 16], P(('slab', 'cross')), may hold values from 0 to 15, each once within a row
Outputs:
- update: float32 [5, 16, 4096], P(None, 'slab', 'cross')
The draws below stay inside these ranges and needn't reach their ends.
Inputs may be any that keep to these rules, and one draw needn't show every extreme that they name: `dinv`: each is s (I + E) with s between 0.5 and 2 a cell and small E. `weights`: positive; the 8 weights of one fringe point sum to one. Among the 1024 fringe points of one device no owner is named more than 128 times.
All inputs are finite; a program needn't handle non-finite values.
Results may differ from the reference program's by a relative error of at most 0.00021.
Values sent between devices are 32-bit elements; how exact they have to be, the bound alone decides.
A program may use at most 64 MiB of HBM per device.

```python
import math
import jax
import jax.numpy as jnp
import numpy as np
from jax import lax

VARIABLES = 5
CORNERS = 8
BLOCK_CELLS = 128
PLANES_DEV = 2
CELLS_DEV = 1024
BLOCKS_DEV = 16
FRINGE_BLOCKS = 8
FRINGE_DEV = 1024
CAPACITY = 128
LAYER_COUNT = 16
COLUMNS = 4096
FRINGE = 32768
N_SLAB = 8
N_CROSS = 4
DEVICES = 32


def cell_scale(key):
    draw = jax.random.uniform(jax.random.fold_in(key, 501), (LAYER_COUNT, COLUMNS), jnp.float32)
    return jnp.exp(jnp.log(0.5) + draw * jnp.log(4.0))


def channel_rates(key, salt):
    first, second, third, fourth = jax.random.split(jax.random.fold_in(key, salt), 4)
    lowest = jnp.log(20.0)
    highest = jnp.log(3.0 * LAYER_COUNT)
    life = jnp.exp(lowest + jax.random.uniform(first, (VARIABLES, 1, 1), jnp.float32) * (highest - lowest))
    life = life * jnp.exp(jax.random.uniform(second, (VARIABLES, LAYER_COUNT, COLUMNS), jnp.float32, -0.35, 0.35))
    damping_factor = jnp.exp(-1.0 / life)
    picked_elements = jax.random.randint(third, (3,), 0, LAYER_COUNT)
    traversal_batch_team = jnp.any(jnp.arange(LAYER_COUNT)[:, None] == picked_elements[None, :], axis=1)
    goal_measure = jax.random.uniform(fourth, (VARIABLES, 1, 1), jnp.float32, 0.5, 0.8)
    return jnp.where(traversal_batch_team[None, :, None], damping_factor * goal_measure, damping_factor)


def small_noise(key, salt):
    return 0.04 * jax.random.truncated_normal(jax.random.fold_in(key, salt), -3.0, 3.0, (VARIABLES, VARIABLES, LAYER_COUNT, COLUMNS), jnp.float32)


def identity_block():
    return jnp.eye(VARIABLES, dtype=jnp.float32)[:, :, None, None]


def draw_dinv(key, part):
    scale = cell_scale(key)
    return scale[None, None] * (identity_block() + small_noise(key, 601))


def draw_lower_jac(key, part):
    scale = cell_scale(key)
    damping_factor = channel_rates(key, 701)
    return (identity_block() * damping_factor[:, None] + small_noise(key, 702)) / scale[None, None]


def draw_upper_jac(key, part):
    scale = cell_scale(key)
    damping_factor = channel_rates(key, 801)
    return (identity_block() * damping_factor[:, None] + small_noise(key, 802)) / scale[None, None]


def draw_weights(key, part):
    raw = jax.random.uniform(jax.random.fold_in(key, 901), (CORNERS, FRINGE), jnp.float32, 0.05, 1.0)
    return raw / jnp.sum(raw, axis=0, keepdims=True)


def with_ends(values, stream_key, least, largest):
    place = [jax.random.randint(jax.random.fold_in(stream_key, axis), (), 0, length) for axis, length in enumerate(values.shape)]
    longest = values.shape.index(max(values.shape))
    beside = place[:longest] + [(place[longest] + 1) % values.shape[longest]] + place[longest + 1:]
    return values.at[tuple(place)].set(least).at[tuple(beside)].set(largest)


def block_scale(rng, dims, pieces, least, high):
    loudness = 1.0
    for axis_at, blocks in pieces:
        heights = jax.random.uniform(jax.random.fold_in(jax.random.fold_in(rng, 6), axis_at), (blocks,), jnp.float32, least / len(pieces), high / len(pieces))
        loudness = loudness * jnp.repeat(jnp.exp(heights), dims[axis_at] // blocks).reshape((-1,) + (1,) * (len(dims) - 1 - axis_at))
    return loudness


def shared_out(key, own, number, rows, count, top, bound, skew):
    sequence = jax.random.permutation(key, count)
    heavy_load, ordinary = shares(count, rows * top, bound, skew, True), shares(count, rows * top, bound, skew, False)
    places = jnp.arange(count)

    def named(tallies, offset_by):
        used = int((tallies > 0).sum())
        fixed = max(1, used // 4)
        passed = fixed + (places - fixed + offset_by * (used - fixed)) % max(1, count - fixed)
        return jnp.zeros((count,), jnp.int32).at[sequence[jnp.where(places < fixed, places, passed)]].set(jnp.asarray(tallies, jnp.int32))

    tallies = jnp.where(number % 4 == 0, named(heavy_load, number // 4), named(ordinary, number - number // 4 - 1))
    mixed = jax.random.permutation(jax.random.fold_in(own, 3), count)
    giver, taker = mixed[0:count // 2 * 2:2], mixed[1:count // 2 * 2:2]
    slack = jnp.minimum(tallies[giver] - 1, bound - tallies[taker]) // 2
    slack = jnp.where((giver == sequence[0]) | (taker == sequence[0]) | (tallies[taker] == 0), 0, jnp.maximum(slack, 0))
    passed = jax.random.randint(jax.random.fold_in(own, 4), (count // 2,), 0, 1 << 20) % (slack + 1)
    tallies = tallies.at[giver].add(-passed).at[taker].add(passed)
    labels = jnp.searchsorted(jnp.cumsum(tallies), jnp.arange(rows * top), side="right").astype(jnp.int32)
    table = labels.reshape(top, rows).T
    table = table[jax.random.permutation(jax.random.fold_in(own, 1), rows)]
    offset_by = jax.random.randint(jax.random.fold_in(own, 2), (rows, 1), 0, top)
    return jnp.take_along_axis(table, (jnp.arange(top)[None, :] + offset_by) % top, axis=1)


def shares(count, total, reach, lean, full):
    loads = [(1 << 20) // math.isqrt(grade ** lean) + 1 for grade in range(1, count + 1)]
    largest = reach if full else min(reach, max(-(-total // count), total * loads[0] // sum(loads)))
    least = 1 if total - largest >= count - 1 else 0
    given, spare = [largest] + [least] * (count - 1), total - largest - least * (count - 1)
    while spare > 0:
        free = [i for i in range(1, count) if given[i] < largest] or [i for i in range(1, count) if given[i] < reach]
        pool, left = sum([loads[i] for i in free]), spare
        for i in free:
            addition = min(reach - given[i], max(1, left * loads[i] // pool), spare)
            given[i] = given[i] + addition
            spare = spare - addition
    return np.array(given)


def scatter_about(key, dims, spread, most, pieces=(), kind=jnp.bfloat16):
    level = block_scale(key, dims, pieces, -0.22, 0.18) if pieces else 1.0
    values = jax.random.normal(key, dims, jnp.float32) * spread * level
    return jnp.minimum(jnp.maximum(values, -most), most).astype(kind)


def setup_inputs(seed: int = 0) -> dict:
    splits = jax.random.split(jax.random.key(seed), 11)
    state = scatter_about(splits[0], (VARIABLES, LAYER_COUNT, COLUMNS), 0.2, 1.2, ((1, 8), (2, 4)), jnp.float32)
    rhs = scatter_about(splits[1], (VARIABLES, LAYER_COUNT, COLUMNS), 0.2, 1.2, ((1, 8), (2, 4)), jnp.float32)
    dinv = draw_dinv(jax.random.fold_in(splits[10], 71), 0)
    lower_jac = draw_lower_jac(jax.random.fold_in(splits[10], 71), 0)
    upper_jac = draw_upper_jac(jax.random.fold_in(splits[10], 71), 0)
    owner_keys = jax.random.split(jax.random.fold_in(splits[5], 1), FRINGE // FRINGE_DEV)
    owner_turns = jax.random.permutation(jax.random.fold_in(splits[5], 3), FRINGE // FRINGE_DEV)
    owner = jax.vmap(lambda own, number: shared_out(jax.random.fold_in(splits[5], 2), own, number, FRINGE_DEV, DEVICES, 1, CAPACITY, 2))(owner_keys, owner_turns).reshape((FRINGE, 1))
    donor_block = with_ends(jax.random.randint(splits[6], (FRINGE,), 0, BLOCKS_DEV), jax.random.fold_in(splits[6], 1), 0, BLOCKS_DEV - 1).astype(jnp.int32)
    offsets = with_ends(jax.random.randint(splits[7], (CORNERS, FRINGE), 0, BLOCK_CELLS), jax.random.fold_in(splits[7], 1), 0, BLOCK_CELLS - 1).astype(jnp.int32)
    weights = draw_weights(jax.random.fold_in(splits[10], 71), 0)
    receptor_perm = jax.vmap(lambda own: jax.random.permutation(own, BLOCKS_DEV))(jax.random.split(splits[9], DEVICES)).reshape((DEVICES, BLOCKS_DEV)).astype(jnp.int32)
    return dict(state=state, rhs=rhs, dinv=dinv, lower_jac=lower_jac, upper_jac=upper_jac, owner=owner, donor_block=donor_block, offsets=offsets, weights=weights, receptor_perm=receptor_perm)


def onto_processors(field):
    width = field.shape[0]
    split = field.reshape(width, N_SLAB, PLANES_DEV, N_CROSS, CELLS_DEV)
    split = split.transpose(0, 1, 3, 2, 4)
    return split.reshape(width, N_SLAB * N_CROSS, PLANES_DEV * CELLS_DEV)


def from_devices(flat):
    width = flat.shape[0]
    split = flat.reshape(width, N_SLAB, N_CROSS, PLANES_DEV, CELLS_DEV)
    split = split.transpose(0, 1, 3, 2, 4)
    return split.reshape(width, LAYER_COUNT, COLUMNS)


def reference(state, rhs, dinv, lower_jac, upper_jac, owner, donor_block, offsets, weights, receptor_perm):
    highest = lax.Precision.HIGHEST
    state_dev = onto_processors(state)
    rhs_dev = onto_processors(rhs)
    donor_owner = owner[:, 0]
    donor_cells = donor_block[None, :] * BLOCK_CELLS + offsets
    values = state_dev[:, donor_owner[None, :], donor_cells]
    interp = jnp.sum(weights[None] * values, axis=1)
    interp = interp.reshape(VARIABLES, DEVICES, FRINGE_DEV)
    starts = receptor_perm[:, :FRINGE_BLOCKS] * BLOCK_CELLS
    targets = (starts[:, :, None] + jnp.arange(BLOCK_CELLS, dtype=jnp.int32)[None, None, :]).reshape(DEVICES, FRINGE_DEV)
    rows = jnp.arange(DEVICES, dtype=jnp.int32)[:, None]
    current = state_dev[:, rows, targets]
    forced = rhs_dev.at[:, rows, targets].set(interp - current)
    forcing = from_devices(forced)

    def planes_first(array):
        return jnp.moveaxis(array, -2, 0)

    def lower_step(prior_iterate, inputs):
        inverse, coupling, source = inputs
        inner = source + jnp.einsum('ijc,jc->ic', coupling, prior_iterate, precision=highest)
        now = jnp.einsum('ijc,jc->ic', inverse, inner, precision=highest)
        return now, now

    start = jnp.zeros((VARIABLES, COLUMNS), jnp.float32)
    _, lower = lax.scan(lower_step, start, (planes_first(dinv), planes_first(lower_jac), planes_first(forcing)))

    def upper_step(following, inputs):
        inverse, coupling, partial_value = inputs
        inner = jnp.einsum('ijc,jc->ic', coupling, following, precision=highest)
        now = partial_value + jnp.einsum('ijc,jc->ic', inverse, inner, precision=highest)
        return now, now

    _, result = lax.scan(upper_step, start, (planes_first(dinv), planes_first(upper_jac), lower), reverse=True)
    return jnp.moveaxis(result, 0, 1)
```

```python
import functools

import jax
import jax.numpy as jnp
from jax import lax
from jax.experimental import pallas as pl
from jax.experimental.pallas import tpu as pltpu
from jax.sharding import PartitionSpec as P

LANES = 128
MAT_ROWS = 80
VEC_ROWS = 16
MESH = pl.DeviceIdType.MESH


def kernel(
    dims,
    state,
    rhs,
    dinv,
    low,
    up,
    owner,
    donor,
    offsets,
    weights,
    perm,
    out,
    gath,
    onehot,
    mask,
    interp,
    mats,
    last,
    vecs,
    mrecv,
    brecv,
    solved,
    entry,
    g_send,
    g_recv,
    m_send,
    m_recv,
    b_send,
    b_recv,
    e_send,
    e_recv,
):
    nz, ny, nx, nc, width, tiles, fringe, corners = dims
    slabs = nz * ny
    solvers = min(tiles, slabs)
    apart = slabs // solvers
    rows = 2 * tiles
    s, c = lax.axis_index("slab"), lax.axis_index("cross")
    z, y = s // ny, lax.rem(s, ny)
    x, w = c // nc, lax.rem(c, nc)

    def at(slab, cross):
        return {"slab": slab, "cross": cross}

    stages = [
        (nz, lambda k: at(lax.rem(z + k, nz) * ny + y, c)),
        (ny, lambda k: at(z * ny + lax.rem(y + k, ny), c)),
        (nx, lambda k: at(s, lax.rem(x + k, nx) * nc + w)),
        (nc, lambda k: at(s, x * nc + lax.rem(w + k, nc))),
    ]

    barrier = pltpu.get_barrier_semaphore()
    peers = [at(lax.rem(s + k, slabs), c) for k in range(1, slabs)]
    for size, peer in stages[2:]:
        peers += [peer(k) for k in range(1, size)]
    for peer in peers:
        pl.semaphore_signal(barrier, inc=1, device_id=peer, device_id_type=MESH)
    pl.semaphore_wait(barrier, len(peers))

    starts = [0, nz, nz + ny, nz + ny + nx]
    views = [
        gath.at[z, y, x, w],
        gath.at[:, y, x, w],
        gath.at[:, :, x, w],
        gath.at[:, :, :, w],
    ]

    def send_stage(number):
        size, peer = stages[number]
        made = []
        for k in range(1, size):
            copy = pltpu.make_async_remote_copy(
                src_ref=state if number == 0 else views[number],
                dst_ref=views[number],
                send_sem=g_send.at[starts[number] + k],
                recv_sem=g_recv.at[starts[number] + k],
                device_id=peer(k),
                device_id_type=MESH,
            )
            copy.start()
            made.append(copy)
        return made

    def finish(made):
        for copy in made:
            copy.wait_recv()

    sent = [send_stage(0)]
    gath[z, y, x, w] = state[...]

    def cell(ref, i, j, p):
        return ref[pl.ds((i * width + j) * rows + p, tiles, stride=2), :]

    def block(ref, p):
        return [[cell(ref, i, j, p) for j in range(width)] for i in range(width)]

    def product(a, b):
        return [
            [sum(a[i][k] * b[k][j] for k in range(width)) for j in range(width)]
            for i in range(width)
        ]

    def keep(ref, stride, base, value):
        ref[pl.ds(base, tiles, stride=stride), :] = value

    def keep_block(number, a):
        for i in range(width):
            for j in range(width):
                keep(mats, MAT_ROWS, number * width * width + j * width + i, a[i][j])

    first_low = product(block(dinv, 0), block(low, 0))
    both_low = product(product(block(dinv, 1), block(low, 1)), first_low)
    keep_block(0, both_low)
    first_up = product(block(dinv, 0), block(up, 0))
    through = product(first_up, both_low)
    keep_block(
        1, [[first_low[i][j] + through[i][j] for j in range(width)] for i in range(width)]
    )
    last_up = product(block(dinv, 1), block(up, 1))
    for i in range(width):
        for j in range(width):
            last[i * width + j] = last_up[i][j]
    keep_block(2, product(first_up, last_up))
    for chunk in range(tiles):
        mats[pl.ds(chunk * MAT_ROWS + 3 * width * width, 5), :] = jnp.zeros(
            (5, LANES), jnp.float32
        )

    def for_solver(act):
        if apart == 1:
            act()
        else:
            pl.when(lax.rem(s, apart) == 0)(act)

    def to_solver(k, source, size, landing, send, receive):
        chunk = lax.rem(s // apart + k, solvers)
        return pltpu.make_async_remote_copy(
            src_ref=source.at[pl.ds(pl.multiple_of(chunk * size, 8), size)],
            dst_ref=landing.at[s],
            send_sem=send.at[k],
            recv_sem=receive.at[s],
            device_id=at(chunk * apart, c),
            device_id_type=MESH,
        )

    def scatter(act, source, size, landing, send, receive):
        for k in range(1, solvers):
            act(to_solver(k, source, size, landing, send, receive))
        if apart > 1:

            @pl.when(lax.rem(s, apart) != 0)
            def _():
                act(to_solver(0, source, size, landing, send, receive))

    def own_chunk(source, size, landing):
        def act():
            own = pl.multiple_of((s // apart) * size, 8)
            landing[s] = source[pl.ds(own, size), :]

        for_solver(act)

    def arrivals(landing, receive):
        for k in range(1, slabs):
            sender = lax.rem(s + k, slabs)
            pltpu.make_async_remote_copy(
                src_ref=landing.at[sender],
                dst_ref=landing.at[sender],
                send_sem=receive.at[sender],
                recv_sem=receive.at[sender],
                device_id=at(sender, c),
                device_id_type=MESH,
            ).wait_recv()

    scatter(lambda copy: copy.start(), mats, MAT_ROWS, mrecv, m_send, m_recv)
    own_chunk(mats, MAT_ROWS, mrecv)

    finish(sent[0])
    sent.append(send_stage(1))

    def fill_mask(i, carry):
        at_cell = lax.broadcasted_iota(jnp.int32, (8, fringe), 0) + i * 8
        total = jnp.zeros((8, fringe), jnp.float32)
        for k in range(corners):
            hit = at_cell == offsets[k : k + 1, :]
            total = total + jnp.where(hit, weights[k : k + 1, :], 0.0)
        mask[pl.ds(pl.multiple_of(i * 8, 8), 8), :] = total
        return carry

    lax.fori_loop(0, LANES // 8, fill_mask, 0)
    finish(sent[1])
    sent.append(send_stage(2))

    blocks = donor[...]
    wanted = owner[...] * rows + (blocks % tiles) * 2 + blocks // tiles

    def fill_onehot(i, carry):
        number = lax.broadcasted_iota(jnp.int32, (16, fringe), 0) + i * 16
        value = jnp.where(number == wanted, 1.0, 0.0).astype(jnp.bfloat16)
        onehot[pl.ds(pl.multiple_of(i * 16, 16), 16), :] = value
        return carry

    count = nz * ny * nx * nc * rows
    lax.fori_loop(0, count // 16, fill_onehot, 0)
    finish(sent[2])
    sent.append(send_stage(3))
    finish(sent[3])

    def interpolate(v, carry):
        table = gath[:, :, :, :, pl.ds(pl.multiple_of(v * rows, 8), rows), :]
        table = table.reshape(count, LANES)
        high = table.astype(jnp.bfloat16)
        rest = (table - high.astype(jnp.float32)).astype(jnp.bfloat16)
        both = jnp.concatenate([high, rest], axis=1)
        picked = lax.dot_general(
            both, onehot[...], (((0,), (0,)), ((), ())), preferred_element_type=jnp.float32
        )
        picked = (picked[:LANES] + picked[LANES:]) * mask[...]
        row = jnp.sum(picked, axis=0, keepdims=True)
        for j in range(fringe // LANES):
            interp[v, j : j + 1, :] = row[:, j * LANES : (j + 1) * LANES]
        return carry

    lax.fori_loop(0, width, interpolate, 0)

    tile = lax.broadcasted_iota(jnp.int32, (tiles, LANES), 0)
    forcing = [[], []]
    for v in range(width):
        fresh = interp[v]
        for p in range(2):
            there = pl.ds(v * rows + p, tiles, stride=2)
            now, value = state[there, :], rhs[there, :]
            for j in range(fringe // LANES):
                hit = tile + p * tiles == perm[0, j]
                value = jnp.where(hit, fresh[j : j + 1, :] - now, value)
            forcing[p].append(value)

    def apply(a, b):
        return [sum(a(i, j) * b[j] for j in range(width)) for i in range(width)]

    def plus(a, b):
        return [i + j for i, j in zip(a, b)]

    def of(ref, p):
        return lambda i, j: cell(ref, i, j, p)

    def kept(number):
        return lambda i, j: mats[
            pl.ds(number * width * width + j * width + i, tiles, stride=MAT_ROWS), :
        ]

    lower_first = apply(of(dinv, 0), forcing[0])
    lower_last = apply(of(dinv, 1), plus(forcing[1], apply(of(low, 1), lower_first)))
    upper_first = plus(lower_first, apply(of(dinv, 0), apply(of(up, 0), lower_last)))
    vecs[...] = jnp.zeros_like(vecs)
    for i in range(width):
        keep(vecs, VEC_ROWS, i, lower_last[i])
        keep(vecs, VEC_ROWS, 8 + i, upper_first[i])
    scatter(lambda copy: copy.start(), vecs, VEC_ROWS, brecv, b_send, b_recv)
    own_chunk(vecs, VEC_ROWS, brecv)

    def to_owner(k):
        target = lax.rem(s + k, slabs)
        return pltpu.make_async_remote_copy(
            src_ref=solved.at[target],
            dst_ref=entry.at[pl.ds(pl.multiple_of((s // apart) * VEC_ROWS, 8), VEC_ROWS)],
            send_sem=e_send.at[k],
            recv_sem=e_recv.at[s // apart],
            device_id=at(target, c),
            device_id_type=MESH,
        )

    def solve():
        arrivals(mrecv, m_recv)
        arrivals(brecv, b_recv)

        def matvec(slab, number, vector):
            base = number * width * width
            return sum(
                mrecv[slab, base + j * width : base + (j + 1) * width, :] * vector[j : j + 1, :]
                for j in range(width)
            )

        solved[...] = jnp.zeros_like(solved)
        value = jnp.zeros((width, LANES), jnp.float32)
        constants = []
        for slab in range(slabs):
            solved[slab, 0:width, :] = value
            constants.append(brecv[slab, 8 : 8 + width, :] + matvec(slab, 1, value))
            value = brecv[slab, 0:width, :] + matvec(slab, 0, value)
        value = jnp.zeros((width, LANES), jnp.float32)
        for slab in reversed(range(slabs)):
            solved[slab, 8 : 8 + width, :] = value
            value = constants[slab] + matvec(slab, 2, value)
        for k in range(1, slabs):
            to_owner(k).start()
        own = pl.multiple_of((s // apart) * VEC_ROWS, 8)
        entry[pl.ds(own, VEC_ROWS), :] = solved[s]

    for_solver(solve)

    def take(j):
        there = entry.at[pl.ds(pl.multiple_of(j * VEC_ROWS, 8), VEC_ROWS)]
        pltpu.make_async_remote_copy(
            src_ref=there,
            dst_ref=there,
            send_sem=e_recv.at[j],
            recv_sem=e_recv.at[j],
            device_id=at(j * apart, c),
            device_id_type=MESH,
        ).wait_recv()

    for k in range(1, solvers):
        take(lax.rem(s // apart + k, solvers))
    if apart > 1:
        pl.when(lax.rem(s, apart) != 0)(lambda: take(s // apart))

    def entries(base):
        return [entry[pl.ds(base + i, tiles, stride=VEC_ROWS), :] for i in range(width)]

    from_below, from_above = entries(0), entries(8)
    result_first = plus(
        upper_first, plus(apply(kept(1), from_below), apply(kept(2), from_above))
    )
    result_last = plus(
        lower_last,
        plus(
            apply(kept(0), from_below),
            apply(lambda i, j: last[i * width + j], from_above),
        ),
    )
    for v in range(width):
        out[pl.ds(v * rows, tiles, stride=2), :] = result_first[v]
        out[pl.ds(v * rows + 1, tiles, stride=2), :] = result_last[v]

    for made in sent:
        for copy in made:
            copy.wait_send()
    scatter(lambda copy: copy.wait_send(), mats, MAT_ROWS, mrecv, m_send, m_recv)
    scatter(lambda copy: copy.wait_send(), vecs, VEC_ROWS, brecv, b_send, b_recv)

    def drain():
        for k in range(1, slabs):
            to_owner(k).wait_send()

    for_solver(drain)


def by_tile(array):
    planes, cells = array.shape[-2:]
    split = array.reshape(-1, planes, cells // LANES, LANES)
    return jnp.swapaxes(split, 1, 2).reshape(-1, LANES)


def body(
    state, rhs, dinv, lower_jac, upper_jac, owner, donor_block, offsets, weights, receptor_perm
):
    width, planes, cells = state.shape
    assert planes == 2 and cells % LANES == 0
    slabs, crosses = lax.axis_size("slab"), lax.axis_size("cross")
    ny = 2 if slabs % 2 == 0 else 1
    nc = 2 if crosses % 2 == 0 else 1
    nz, nx = slabs // ny, crosses // nc
    tiles = cells // LANES
    solvers = min(tiles, slabs)
    assert solvers == tiles and slabs % solvers == 0
    rows = planes * tiles
    corners, fringe = offsets.shape
    dims = (nz, ny, nx, nc, width, tiles, fringe, corners)
    f32 = jnp.float32
    vmem = pl.BlockSpec(memory_space=pltpu.VMEM)
    dma = pltpu.SemaphoreType.DMA
    made = pl.pallas_call(
        functools.partial(kernel, dims),
        out_shape=jax.ShapeDtypeStruct((width * rows, LANES), f32),
        in_specs=[vmem] * 9 + [pl.BlockSpec(memory_space=pltpu.SMEM)],
        out_specs=vmem,
        scratch_shapes=[
            pltpu.VMEM((nz, ny, nx, nc, width * rows, LANES), f32),
            pltpu.VMEM((slabs * crosses * rows, fringe), jnp.bfloat16),
            pltpu.VMEM((LANES, fringe), f32),
            pltpu.VMEM((width, fringe // LANES, LANES), f32),
            pltpu.VMEM((tiles * MAT_ROWS, LANES), f32),
            pltpu.VMEM((width * width, tiles, LANES), f32),
            pltpu.VMEM((tiles * VEC_ROWS, LANES), f32),
            pltpu.VMEM((slabs, MAT_ROWS, LANES), f32),
            pltpu.VMEM((slabs, VEC_ROWS, LANES), f32),
            pltpu.VMEM((slabs, VEC_ROWS, LANES), f32),
            pltpu.VMEM((tiles * VEC_ROWS, LANES), f32),
            dma((nz + ny + nx + nc,)),
            dma((nz + ny + nx + nc,)),
            dma((solvers,)),
            dma((slabs,)),
            dma((solvers,)),
            dma((slabs,)),
            dma((slabs,)),
            dma((solvers,)),
        ],
        compiler_params=pltpu.CompilerParams(
            collective_id=0, has_side_effects=True, vmem_limit_bytes=40 * 2**20
        ),
    )(
        by_tile(state),
        by_tile(rhs),
        by_tile(dinv),
        by_tile(lower_jac),
        by_tile(upper_jac),
        owner.reshape(1, fringe),
        donor_block.reshape(1, fringe),
        offsets,
        weights,
        receptor_perm,
    )
    made = jnp.swapaxes(made.reshape(width, tiles, planes, LANES), 1, 2)
    return made.reshape(width, planes, cells)


def solution(mesh):
    whole = ("slab", "cross")
    return jax.shard_map(
        body,
        mesh=mesh,
        in_specs=(
            P(None, "slab", "cross"),
            P(None, "slab", "cross"),
            P(None, None, "slab", "cross"),
            P(None, None, "slab", "cross"),
            P(None, None, "slab", "cross"),
            P(whole, None),
            P(whole),
            P(None, whole),
            P(None, whole),
            P(whole, None),
        ),
        out_specs=P(None, "slab", "cross"),
        check_vma=False,
    )
```

```python
import functools

import jax
import jax.numpy as jnp
from jax import lax
from jax.experimental import pallas as pl
from jax.experimental.pallas import tpu as pltpu
from jax.sharding import PartitionSpec as P

LANES = 128
MAT_ROWS = 80
VEC_ROWS = 16
MESH = pl.DeviceIdType.MESH


def kernel(
    dims,
    *refs,
):
    sources, (out,), scratch = refs[:10], refs[10:11], refs[11:]
    held, f_sem, scratch = scratch[:10], scratch[10], scratch[11:]
    state, rhs, dinv, low, up, owner, donor, offsets, weights, perm = held
    (
    gath,
    onehot,
    mask,
    interp,
    mats,
    last,
    vecs,
    mrecv,
    brecv,
    solved,
    entry,
    g_send,
    g_recv,
    m_send,
    m_recv,
    b_send,
    b_recv,
    e_send,
    e_recv,
    ) = scratch
    nz, ny, nx, nc, width, tiles, fringe, corners = dims
    slabs = nz * ny
    solvers = min(tiles, slabs)
    apart = slabs // solvers
    rows = 2 * tiles
    s, c = lax.axis_index("slab"), lax.axis_index("cross")
    z, y = s // ny, lax.rem(s, ny)
    x, w = c // nc, lax.rem(c, nc)

    def at(slab, cross):
        return {"slab": slab, "cross": cross}

    z_peer = lambda k: at(lax.rem(z + k, nz) * ny + y, c)
    y_peer = lambda k: at(z * ny + lax.rem(y + k, ny), c)
    x_peer = lambda k: at(s, lax.rem(x + k, nx) * nc + w)
    w_peer = lambda k: at(s, x * nc + lax.rem(w + k, nc))

    fetches = [
        pltpu.make_async_copy(source, target, f_sem.at[number])
        for number, (source, target) in enumerate(zip(sources, held))
    ]
    for fetch in fetches:
        fetch.start()

    barrier = pltpu.get_barrier_semaphore()
    peers = [at(lax.rem(s + k, slabs), c) for k in range(1, slabs)]
    peers += [x_peer(k) for k in range(1, nx)] + [w_peer(k) for k in range(1, nc)]
    for peer in peers:
        pl.semaphore_signal(barrier, inc=1, device_id=peer, device_id_type=MESH)
    fetches[0].wait()
    pl.semaphore_wait(barrier, len(peers))

    half = width * rows // 2
    first, second = pl.ds(0, half), pl.ds(half, half)
    sent = []

    def send(size, peer, source, landing):
        made = []
        for k in range(1, size):
            slot = len(sent)
            copy = pltpu.make_async_remote_copy(
                src_ref=source,
                dst_ref=landing,
                send_sem=g_send.at[slot],
                recv_sem=g_recv.at[slot],
                device_id=peer(k),
                device_id_type=MESH,
            )
            copy.start()
            made.append(copy)
            sent.append(copy)
        return made

    def pass_on(size, peer, view):
        return send(size, peer, view, view)

    def finish(made):
        for copy in made:
            copy.wait_recv()

    along_z = send(nz, z_peer, state, gath.at[w, z, y, x])
    gath[w, z, y, x] = state[...]
    for fetch in fetches[1:5]:
        fetch.wait()

    def cell(ref, i, j, p):
        return ref[pl.ds((i * width + j) * rows + p, tiles, stride=2), :]

    def block(ref, p):
        return [[cell(ref, i, j, p) for j in range(width)] for i in range(width)]

    def product(a, b):
        return [
            [sum(a[i][k] * b[k][j] for k in range(width)) for j in range(width)]
            for i in range(width)
        ]

    def keep(ref, stride, base, value):
        ref[pl.ds(base, tiles, stride=stride), :] = value

    def keep_block(number, a):
        for i in range(width):
            for j in range(width):
                keep(mats, MAT_ROWS, number * width * width + j * width + i, a[i][j])

    first_low = product(block(dinv, 0), block(low, 0))
    both_low = product(product(block(dinv, 1), block(low, 1)), first_low)
    keep_block(0, both_low)
    first_up = product(block(dinv, 0), block(up, 0))
    through = product(first_up, both_low)
    keep_block(
        1, [[first_low[i][j] + through[i][j] for j in range(width)] for i in range(width)]
    )
    last_up = product(block(dinv, 1), block(up, 1))
    for i in range(width):
        for j in range(width):
            last[i * width + j] = last_up[i][j]
    keep_block(2, product(first_up, last_up))
    for chunk in range(tiles):
        mats[pl.ds(chunk * MAT_ROWS + 3 * width * width, 5), :] = jnp.zeros(
            (5, LANES), jnp.float32
        )

    def for_solver(act):
        if apart == 1:
            act()
        else:
            pl.when(lax.rem(s, apart) == 0)(act)

    def to_solver(k, source, size, landing, send, receive):
        chunk = lax.rem(s // apart + k, solvers)
        return pltpu.make_async_remote_copy(
            src_ref=source.at[pl.ds(pl.multiple_of(chunk * size, 8), size)],
            dst_ref=landing.at[s],
            send_sem=send.at[k],
            recv_sem=receive.at[s],
            device_id=at(chunk * apart, c),
            device_id_type=MESH,
        )

    def scatter(act, source, size, landing, send, receive):
        for k in range(1, solvers):
            act(to_solver(k, source, size, landing, send, receive))
        if apart > 1:

            @pl.when(lax.rem(s, apart) != 0)
            def _():
                act(to_solver(0, source, size, landing, send, receive))

    def own_chunk(source, size, landing):
        def act():
            own = pl.multiple_of((s // apart) * size, 8)
            landing[s] = source[pl.ds(own, size), :]

        for_solver(act)

    def arrivals(landing, receive):
        for k in range(1, slabs):
            sender = lax.rem(s + k, slabs)
            pltpu.make_async_remote_copy(
                src_ref=landing.at[sender],
                dst_ref=landing.at[sender],
                send_sem=receive.at[sender],
                recv_sem=receive.at[sender],
                device_id=at(sender, c),
                device_id_type=MESH,
            ).wait_recv()

    own_chunk(mats, MAT_ROWS, mrecv)

    finish(along_z)
    first_y = pass_on(ny, y_peer, gath.at[w, :, y, x, first])
    second_x = pass_on(nx, x_peer, gath.at[w, :, y, x, second])
    for fetch in fetches[5:]:
        fetch.wait()

    def fill_mask(i, carry):
        at_cell = lax.broadcasted_iota(jnp.int32, (8, fringe), 0) + i * 8
        total = jnp.zeros((8, fringe), jnp.float32)
        for k in range(corners):
            hit = at_cell == offsets[k : k + 1, :]
            total = total + jnp.where(hit, weights[k : k + 1, :], 0.0)
        mask[pl.ds(pl.multiple_of(i * 8, 8), 8), :] = total
        return carry

    lax.fori_loop(0, LANES // 8, fill_mask, 0)
    finish(first_y)
    first_x = pass_on(nx, x_peer, gath.at[w, :, :, x, first])
    finish(second_x)
    second_y = pass_on(ny, y_peer, gath.at[w, :, y, :, second])
    scatter(lambda copy: copy.start(), mats, MAT_ROWS, mrecv, m_send, m_recv)

    blocks = donor[...]
    group = nz * ny * nx
    place = (owner[...] % nc) * group + owner[...] // nc
    wanted = place * rows + (blocks % tiles) * 2 + blocks // tiles

    def fill_onehot(i, carry):
        number = lax.broadcasted_iota(jnp.int32, (16, fringe), 0) + i * 16
        value = jnp.where(number == wanted, 1.0, 0.0).astype(jnp.bfloat16)
        onehot[pl.ds(pl.multiple_of(i * 16, 16), 16), :] = value
        return carry

    count = nz * ny * nx * nc * rows
    lax.fori_loop(0, count // 16, fill_onehot, 0)
    finish(second_y)
    by_core = pass_on(nc, w_peer, gath.at[w, :, :, :, second])
    finish(first_x)
    by_core += pass_on(nc, w_peer, gath.at[w, :, :, :, first])

    part = group * rows

    def interpolate(core, add, v, carry):
        table = gath[core, :, :, :, pl.ds(pl.multiple_of(v * rows, 8), rows), :]
        table = table.reshape(part, LANES)
        high = table.astype(jnp.bfloat16)
        rest = (table - high.astype(jnp.float32)).astype(jnp.bfloat16)
        chosen = onehot[pl.ds(pl.multiple_of(core * part, 16), part), :]
        both = jnp.concatenate([high, rest], axis=1)
        picked = lax.dot_general(
            both, chosen, (((0,), (0,)), ((), ())), preferred_element_type=jnp.float32
        )
        picked = (picked[:LANES] + picked[LANES:]) * mask[...]
        row = jnp.sum(picked, axis=0, keepdims=True)
        for j in range(fringe // LANES):
            value = row[:, j * LANES : (j + 1) * LANES]
            interp[v, j : j + 1, :] = interp[v, j : j + 1, :] + value if add else value
        return carry

    lax.fori_loop(0, width, functools.partial(interpolate, w, False), 0)
    finish(by_core)
    for k in range(1, nc):
        core = lax.rem(w + k, nc)
        lax.fori_loop(0, width, functools.partial(interpolate, core, True), 0)

    tile = lax.broadcasted_iota(jnp.int32, (tiles, LANES), 0)
    forcing = [[], []]
    for v in range(width):
        fresh = interp[v]
        for p in range(2):
            there = pl.ds(v * rows + p, tiles, stride=2)
            now, value = state[there, :], rhs[there, :]
            for j in range(fringe // LANES):
                hit = tile + p * tiles == perm[0, j]
                value = jnp.where(hit, fresh[j : j + 1, :] - now, value)
            forcing[p].append(value)

    def apply(a, b):
        return [sum(a(i, j) * b[j] for j in range(width)) for i in range(width)]

    def plus(a, b):
        return [i + j for i, j in zip(a, b)]

    def of(ref, p):
        return lambda i, j: cell(ref, i, j, p)

    def kept(number):
        return lambda i, j: mats[
            pl.ds(number * width * width + j * width + i, tiles, stride=MAT_ROWS), :
        ]

    lower_first = apply(of(dinv, 0), forcing[0])
    lower_last = apply(of(dinv, 1), plus(forcing[1], apply(of(low, 1), lower_first)))
    upper_first = plus(lower_first, apply(of(dinv, 0), apply(of(up, 0), lower_last)))
    vecs[...] = jnp.zeros_like(vecs)
    for i in range(width):
        keep(vecs, VEC_ROWS, i, lower_last[i])
        keep(vecs, VEC_ROWS, 8 + i, upper_first[i])
    scatter(lambda copy: copy.start(), vecs, VEC_ROWS, brecv, b_send, b_recv)
    own_chunk(vecs, VEC_ROWS, brecv)

    def to_owner(k):
        target = lax.rem(s + k, slabs)
        return pltpu.make_async_remote_copy(
            src_ref=solved.at[target],
            dst_ref=entry.at[pl.ds(pl.multiple_of((s // apart) * VEC_ROWS, 8), VEC_ROWS)],
            send_sem=e_send.at[k],
            recv_sem=e_recv.at[s // apart],
            device_id=at(target, c),
            device_id_type=MESH,
        )

    def solve():
        arrivals(mrecv, m_recv)
        arrivals(brecv, b_recv)

        def matvec(slab, number, vector):
            base = number * width * width
            return sum(
                mrecv[slab, base + j * width : base + (j + 1) * width, :] * vector[j : j + 1, :]
                for j in range(width)
            )

        solved[...] = jnp.zeros_like(solved)
        value = jnp.zeros((width, LANES), jnp.float32)
        constants = []
        for slab in range(slabs):
            solved[slab, 0:width, :] = value
            constants.append(brecv[slab, 8 : 8 + width, :] + matvec(slab, 1, value))
            value = brecv[slab, 0:width, :] + matvec(slab, 0, value)
        value = jnp.zeros((width, LANES), jnp.float32)
        for slab in reversed(range(slabs)):
            solved[slab, 8 : 8 + width, :] = value
            value = constants[slab] + matvec(slab, 2, value)
        for k in range(1, slabs):
            to_owner(k).start()
        own = pl.multiple_of((s // apart) * VEC_ROWS, 8)
        entry[pl.ds(own, VEC_ROWS), :] = solved[s]

    for_solver(solve)

    def take(j):
        there = entry.at[pl.ds(pl.multiple_of(j * VEC_ROWS, 8), VEC_ROWS)]
        pltpu.make_async_remote_copy(
            src_ref=there,
            dst_ref=there,
            send_sem=e_recv.at[j],
            recv_sem=e_recv.at[j],
            device_id=at(j * apart, c),
            device_id_type=MESH,
        ).wait_recv()

    for k in range(1, solvers):
        take(lax.rem(s // apart + k, solvers))
    if apart > 1:
        pl.when(lax.rem(s, apart) != 0)(lambda: take(s // apart))

    def entries(base):
        return [entry[pl.ds(base + i, tiles, stride=VEC_ROWS), :] for i in range(width)]

    from_below, from_above = entries(0), entries(8)
    result_first = plus(
        upper_first, plus(apply(kept(1), from_below), apply(kept(2), from_above))
    )
    result_last = plus(
        lower_last,
        plus(
            apply(kept(0), from_below),
            apply(lambda i, j: last[i * width + j], from_above),
        ),
    )
    for v in range(width):
        out[pl.ds(v * rows, tiles, stride=2), :] = result_first[v]
        out[pl.ds(v * rows + 1, tiles, stride=2), :] = result_last[v]

    for copy in sent:
        copy.wait_send()
    scatter(lambda copy: copy.wait_send(), mats, MAT_ROWS, mrecv, m_send, m_recv)
    scatter(lambda copy: copy.wait_send(), vecs, VEC_ROWS, brecv, b_send, b_recv)

    def drain():
        for k in range(1, slabs):
            to_owner(k).wait_send()

    for_solver(drain)


def by_tile(array):
    planes, cells = array.shape[-2:]
    split = array.reshape(-1, planes, cells // LANES, LANES)
    return jnp.swapaxes(split, 1, 2).reshape(-1, LANES)


def body(
    state, rhs, dinv, lower_jac, upper_jac, owner, donor_block, offsets, weights, receptor_perm
):
    width, planes, cells = state.shape
    assert planes == 2 and cells % LANES == 0
    slabs, crosses = lax.axis_size("slab"), lax.axis_size("cross")
    ny = 2 if slabs % 2 == 0 else 1
    nc = 2 if crosses % 2 == 0 else 1
    nz, nx = slabs // ny, crosses // nc
    tiles = cells // LANES
    solvers = min(tiles, slabs)
    assert solvers == tiles and slabs % solvers == 0
    rows = planes * tiles
    corners, fringe = offsets.shape
    dims = (nz, ny, nx, nc, width, tiles, fringe, corners)
    f32 = jnp.float32
    vmem = pl.BlockSpec(memory_space=pltpu.VMEM)
    dma = pltpu.SemaphoreType.DMA
    copies = (nz - 1) + 2 * (ny + nx + nc - 3)
    operands = (
        by_tile(state),
        by_tile(rhs),
        by_tile(dinv),
        by_tile(lower_jac),
        by_tile(upper_jac),
        owner.reshape(1, fringe),
        donor_block.reshape(1, fringe),
        offsets,
        weights,
        receptor_perm,
    )
    made = pl.pallas_call(
        functools.partial(kernel, dims),
        out_shape=jax.ShapeDtypeStruct((width * rows, LANES), f32),
        in_specs=[pl.BlockSpec(memory_space=pltpu.HBM)] * 10,
        out_specs=vmem,
        scratch_shapes=[
            *(pltpu.VMEM(a.shape, a.dtype) for a in operands[:-1]),
            pltpu.SMEM(receptor_perm.shape, receptor_perm.dtype),
            dma((len(operands),)),
            pltpu.VMEM((nc, nz, ny, nx, width * rows, LANES), f32),
            pltpu.VMEM((slabs * crosses * rows, fringe), jnp.bfloat16),
            pltpu.VMEM((LANES, fringe), f32),
            pltpu.VMEM((width, fringe // LANES, LANES), f32),
            pltpu.VMEM((tiles * MAT_ROWS, LANES), f32),
            pltpu.VMEM((width * width, tiles, LANES), f32),
            pltpu.VMEM((tiles * VEC_ROWS, LANES), f32),
            pltpu.VMEM((slabs, MAT_ROWS, LANES), f32),
            pltpu.VMEM((slabs, VEC_ROWS, LANES), f32),
            pltpu.VMEM((slabs, VEC_ROWS, LANES), f32),
            pltpu.VMEM((tiles * VEC_ROWS, LANES), f32),
            dma((copies,)),
            dma((copies,)),
            dma((solvers,)),
            dma((slabs,)),
            dma((solvers,)),
            dma((slabs,)),
            dma((slabs,)),
            dma((solvers,)),
        ],
        compiler_params=pltpu.CompilerParams(
            collective_id=0, has_side_effects=True, vmem_limit_bytes=62 * 2**20
        ),
    )(*operands)
    made = jnp.swapaxes(made.reshape(width, tiles, planes, LANES), 1, 2)
    return made.reshape(width, planes, cells)


def solution(mesh):
    whole = ("slab", "cross")
    return jax.shard_map(
        body,
        mesh=mesh,
        in_specs=(
            P(None, "slab", "cross"),
            P(None, "slab", "cross"),
            P(None, None, "slab", "cross"),
            P(None, None, "slab", "cross"),
            P(None, None, "slab", "cross"),
            P(whole, None),
            P(whole),
            P(None, whole),
            P(None, whole),
            P(whole, None),
        ),
        out_specs=P(None, "slab", "cross"),
        check_vma=False,
    )
```

```python
import functools

import jax
import jax.numpy as jnp
from jax import lax
from jax.experimental import pallas as pl
from jax.experimental.pallas import tpu as pltpu
from jax.sharding import PartitionSpec as P

LANES = 128
MAT_ROWS = 80
VEC_ROWS = 16
MESH = pl.DeviceIdType.MESH


def kernel(
    dims,
    *refs,
):
    sources, (out,), scratch = refs[:10], refs[10:11], refs[11:]
    held, f_sem, scratch = scratch[:10], scratch[10], scratch[11:]
    state, rhs, dinv, low, up, owner, donor, offsets, weights, perm = held
    (
    gath,
    onehot,
    mask,
    interp,
    mats,
    last,
    vecs,
    mrecv,
    brecv,
    solved,
    entry,
    g_send,
    g_recv,
    m_send,
    m_recv,
    b_send,
    b_recv,
    e_send,
    e_recv,
    ) = scratch
    nz, ny, nx, nc, width, tiles, fringe, corners = dims
    slabs = nz * ny
    solvers = min(tiles, slabs)
    apart = slabs // solvers
    rows = 2 * tiles
    s, c = lax.axis_index("slab"), lax.axis_index("cross")
    z, y = s // ny, lax.rem(s, ny)
    x, w = c // nc, lax.rem(c, nc)

    def at(slab, cross):
        return {"slab": slab, "cross": cross}

    z_peer = lambda k: at(lax.rem(z + k, nz) * ny + y, c)
    y_peer = lambda k: at(z * ny + lax.rem(y + k, ny), c)
    x_peer = lambda k: at(s, lax.rem(x + k, nx) * nc + w)
    w_peer = lambda k: at(s, x * nc + lax.rem(w + k, nc))

    fetches = [
        pltpu.make_async_copy(source, target, f_sem.at[number])
        for number, (source, target) in enumerate(zip(sources, held))
    ]
    for fetch in fetches:
        fetch.start()

    barrier = pltpu.get_barrier_semaphore()
    peers = [at(lax.rem(s + k, slabs), c) for k in range(1, slabs)]
    peers += [x_peer(k) for k in range(1, nx)] + [w_peer(k) for k in range(1, nc)]
    for peer in peers:
        pl.semaphore_signal(barrier, inc=1, device_id=peer, device_id_type=MESH)
    fetches[0].wait()
    pl.semaphore_wait(barrier, len(peers))

    half = width * rows // 2
    first, second = pl.ds(0, half), pl.ds(half, half)
    sent = []

    def send(size, peer, source, landing):
        made = []
        for k in range(1, size):
            slot = len(sent)
            copy = pltpu.make_async_remote_copy(
                src_ref=source,
                dst_ref=landing,
                send_sem=g_send.at[slot],
                recv_sem=g_recv.at[slot],
                device_id=peer(k),
                device_id_type=MESH,
            )
            copy.start()
            made.append(copy)
            sent.append(copy)
        return made

    def pass_on(size, peer, view):
        return send(size, peer, view, view)

    def finish(made):
        for copy in made:
            copy.wait_recv()

    along_z = send(nz, z_peer, state, gath.at[w, z, y, x])
    gath[w, z, y, x] = state[...]
    for fetch in fetches[1:5]:
        fetch.wait()

    def cell(ref, i, j, p):
        return ref[pl.ds((i * width + j) * rows + p, tiles, stride=2), :]

    def block(ref, p):
        return [[cell(ref, i, j, p) for j in range(width)] for i in range(width)]

    def product(a, b):
        return [
            [sum(a[i][k] * b[k][j] for k in range(width)) for j in range(width)]
            for i in range(width)
        ]

    def keep(ref, stride, base, value):
        ref[pl.ds(base, tiles, stride=stride), :] = value

    def keep_block(number, a):
        for i in range(width):
            for j in range(width):
                keep(mats, MAT_ROWS, number * width * width + j * width + i, a[i][j])

    first_low = product(block(dinv, 0), block(low, 0))
    both_low = product(product(block(dinv, 1), block(low, 1)), first_low)
    keep_block(0, both_low)
    first_up = product(block(dinv, 0), block(up, 0))
    through = product(first_up, both_low)
    keep_block(
        1, [[first_low[i][j] + through[i][j] for j in range(width)] for i in range(width)]
    )
    last_up = product(block(dinv, 1), block(up, 1))
    for i in range(width):
        for j in range(width):
            last[i * width + j] = last_up[i][j]
    keep_block(2, product(first_up, last_up))
    for chunk in range(tiles):
        mats[pl.ds(chunk * MAT_ROWS + 3 * width * width, 5), :] = jnp.zeros(
            (5, LANES), jnp.float32
        )

    def for_solver(act):
        if apart == 1:
            act()
        else:
            pl.when(lax.rem(s, apart) == 0)(act)

    def to_solver(k, source, size, landing, send, receive):
        chunk = lax.rem(s // apart + k, solvers)
        return pltpu.make_async_remote_copy(
            src_ref=source.at[pl.ds(pl.multiple_of(chunk * size, 8), size)],
            dst_ref=landing.at[s],
            send_sem=send.at[k],
            recv_sem=receive.at[s],
            device_id=at(chunk * apart, c),
            device_id_type=MESH,
        )

    def scatter(act, source, size, landing, send, receive):
        for k in range(1, solvers):
            act(to_solver(k, source, size, landing, send, receive))
        if apart > 1:

            @pl.when(lax.rem(s, apart) != 0)
            def _():
                act(to_solver(0, source, size, landing, send, receive))

    def own_chunk(source, size, landing):
        def act():
            own = pl.multiple_of((s // apart) * size, 8)
            landing[s] = source[pl.ds(own, size), :]

        for_solver(act)

    def arrivals(landing, receive):
        for k in range(1, slabs):
            sender = lax.rem(s + k, slabs)
            pltpu.make_async_remote_copy(
                src_ref=landing.at[sender],
                dst_ref=landing.at[sender],
                send_sem=receive.at[sender],
                recv_sem=receive.at[sender],
                device_id=at(sender, c),
                device_id_type=MESH,
            ).wait_recv()

    own_chunk(mats, MAT_ROWS, mrecv)

    finish(along_z)
    first_y = pass_on(ny, y_peer, gath.at[w, :, y, x, first])
    second_x = pass_on(nx, x_peer, gath.at[w, :, y, x, second])
    for fetch in fetches[5:]:
        fetch.wait()

    def fill_mask(i, carry):
        at_cell = lax.broadcasted_iota(jnp.int32, (8, fringe), 0) + i * 8
        total = jnp.zeros((8, fringe), jnp.float32)
        for k in range(corners):
            hit = at_cell == offsets[k : k + 1, :]
            total = total + jnp.where(hit, weights[k : k + 1, :], 0.0)
        mask[pl.ds(pl.multiple_of(i * 8, 8), 8), :] = total
        return carry

    lax.fori_loop(0, LANES // 8, fill_mask, 0)
    finish(first_y)
    first_x = pass_on(nx, x_peer, gath.at[w, :, :, x, first])
    finish(second_x)
    second_y = pass_on(ny, y_peer, gath.at[w, :, y, :, second])

    blocks = donor[...]
    group = nz * ny * nx
    place = (owner[...] % nc) * group + owner[...] // nc
    wanted = place * rows + (blocks % tiles) * 2 + blocks // tiles

    def fill_onehot(i, carry):
        number = lax.broadcasted_iota(jnp.int32, (16, fringe), 0) + i * 16
        value = jnp.where(number == wanted, 1.0, 0.0).astype(jnp.bfloat16)
        onehot[pl.ds(pl.multiple_of(i * 16, 16), 16), :] = value
        return carry

    count = nz * ny * nx * nc * rows
    lax.fori_loop(0, count // 16, fill_onehot, 0)
    finish(second_y)
    by_core = pass_on(nc, w_peer, gath.at[w, :, :, :, second])
    finish(first_x)
    by_core += pass_on(nc, w_peer, gath.at[w, :, :, :, first])
    scatter(lambda copy: copy.start(), mats, MAT_ROWS, mrecv, m_send, m_recv)

    part = group * rows

    def interpolate(core, add, v, carry):
        table = gath[core, :, :, :, pl.ds(pl.multiple_of(v * rows, 8), rows), :]
        table = table.reshape(part, LANES)
        high = table.astype(jnp.bfloat16)
        rest = (table - high.astype(jnp.float32)).astype(jnp.bfloat16)
        chosen = onehot[pl.ds(pl.multiple_of(core * part, 16), part), :]
        both = jnp.concatenate([high, rest], axis=1)
        picked = lax.dot_general(
            both, chosen, (((0,), (0,)), ((), ())), preferred_element_type=jnp.float32
        )
        picked = (picked[:LANES] + picked[LANES:]) * mask[...]
        row = jnp.sum(picked, axis=0, keepdims=True)
        for j in range(fringe // LANES):
            value = row[:, j * LANES : (j + 1) * LANES]
            interp[v, j : j + 1, :] = interp[v, j : j + 1, :] + value if add else value
        return carry

    lax.fori_loop(0, width, functools.partial(interpolate, w, False), 0)
    finish(by_core)
    for k in range(1, nc):
        core = lax.rem(w + k, nc)
        lax.fori_loop(0, width, functools.partial(interpolate, core, True), 0)

    tile = lax.broadcasted_iota(jnp.int32, (tiles, LANES), 0)
    forcing = [[], []]
    for v in range(width):
        fresh = interp[v]
        for p in range(2):
            there = pl.ds(v * rows + p, tiles, stride=2)
            now, value = state[there, :], rhs[there, :]
            for j in range(fringe // LANES):
                hit = tile + p * tiles == perm[0, j]
                value = jnp.where(hit, fresh[j : j + 1, :] - now, value)
            forcing[p].append(value)

    def apply(a, b):
        return [sum(a(i, j) * b[j] for j in range(width)) for i in range(width)]

    def plus(a, b):
        return [i + j for i, j in zip(a, b)]

    def of(ref, p):
        return lambda i, j: cell(ref, i, j, p)

    def kept(number):
        return lambda i, j: mats[
            pl.ds(number * width * width + j * width + i, tiles, stride=MAT_ROWS), :
        ]

    lower_first = apply(of(dinv, 0), forcing[0])
    lower_last = apply(of(dinv, 1), plus(forcing[1], apply(of(low, 1), lower_first)))
    upper_first = plus(lower_first, apply(of(dinv, 0), apply(of(up, 0), lower_last)))
    vecs[...] = jnp.zeros_like(vecs)
    for i in range(width):
        keep(vecs, VEC_ROWS, i, lower_last[i])
        keep(vecs, VEC_ROWS, 8 + i, upper_first[i])
    scatter(lambda copy: copy.start(), vecs, VEC_ROWS, brecv, b_send, b_recv)
    own_chunk(vecs, VEC_ROWS, brecv)

    def to_owner(k):
        target = lax.rem(s + k, slabs)
        return pltpu.make_async_remote_copy(
            src_ref=solved.at[target],
            dst_ref=entry.at[pl.ds(pl.multiple_of((s // apart) * VEC_ROWS, 8), VEC_ROWS)],
            send_sem=e_send.at[k],
            recv_sem=e_recv.at[s // apart],
            device_id=at(target, c),
            device_id_type=MESH,
        )

    def solve():
        arrivals(mrecv, m_recv)
        arrivals(brecv, b_recv)

        def matvec(slab, number, vector):
            base = number * width * width
            return sum(
                mrecv[slab, base + j * width : base + (j + 1) * width, :] * vector[j : j + 1, :]
                for j in range(width)
            )

        solved[...] = jnp.zeros_like(solved)
        value = jnp.zeros((width, LANES), jnp.float32)
        constants = []
        for slab in range(slabs):
            solved[slab, 0:width, :] = value
            constants.append(brecv[slab, 8 : 8 + width, :] + matvec(slab, 1, value))
            value = brecv[slab, 0:width, :] + matvec(slab, 0, value)
        value = jnp.zeros((width, LANES), jnp.float32)
        for slab in reversed(range(slabs)):
            solved[slab, 8 : 8 + width, :] = value
            value = constants[slab] + matvec(slab, 2, value)
        for k in range(1, slabs):
            to_owner(k).start()
        own = pl.multiple_of((s // apart) * VEC_ROWS, 8)
        entry[pl.ds(own, VEC_ROWS), :] = solved[s]

    for_solver(solve)

    def take(j):
        there = entry.at[pl.ds(pl.multiple_of(j * VEC_ROWS, 8), VEC_ROWS)]
        pltpu.make_async_remote_copy(
            src_ref=there,
            dst_ref=there,
            send_sem=e_recv.at[j],
            recv_sem=e_recv.at[j],
            device_id=at(j * apart, c),
            device_id_type=MESH,
        ).wait_recv()

    for k in range(1, solvers):
        take(lax.rem(s // apart + k, solvers))
    if apart > 1:
        pl.when(lax.rem(s, apart) != 0)(lambda: take(s // apart))

    def entries(base):
        return [entry[pl.ds(base + i, tiles, stride=VEC_ROWS), :] for i in range(width)]

    from_below, from_above = entries(0), entries(8)
    result_first = plus(
        upper_first, plus(apply(kept(1), from_below), apply(kept(2), from_above))
    )
    result_last = plus(
        lower_last,
        plus(
            apply(kept(0), from_below),
            apply(lambda i, j: last[i * width + j], from_above),
        ),
    )
    for v in range(width):
        out[pl.ds(v * rows, tiles, stride=2), :] = result_first[v]
        out[pl.ds(v * rows + 1, tiles, stride=2), :] = result_last[v]

    for copy in sent:
        copy.wait_send()
    scatter(lambda copy: copy.wait_send(), mats, MAT_ROWS, mrecv, m_send, m_recv)
    scatter(lambda copy: copy.wait_send(), vecs, VEC_ROWS, brecv, b_send, b_recv)

    def drain():
        for k in range(1, slabs):
            to_owner(k).wait_send()

    for_solver(drain)


def by_tile(array):
    planes, cells = array.shape[-2:]
    split = array.reshape(-1, planes, cells // LANES, LANES)
    return jnp.swapaxes(split, 1, 2).reshape(-1, LANES)


def body(
    state, rhs, dinv, lower_jac, upper_jac, owner, donor_block, offsets, weights, receptor_perm
):
    width, planes, cells = state.shape
    assert planes == 2 and cells % LANES == 0
    slabs, crosses = lax.axis_size("slab"), lax.axis_size("cross")
    ny = 2 if slabs % 2 == 0 else 1
    nc = 2 if crosses % 2 == 0 else 1
    nz, nx = slabs // ny, crosses // nc
    tiles = cells // LANES
    solvers = min(tiles, slabs)
    assert solvers == tiles and slabs % solvers == 0
    rows = planes * tiles
    corners, fringe = offsets.shape
    dims = (nz, ny, nx, nc, width, tiles, fringe, corners)
    f32 = jnp.float32
    vmem = pl.BlockSpec(memory_space=pltpu.VMEM)
    dma = pltpu.SemaphoreType.DMA
    copies = (nz - 1) + 2 * (ny + nx + nc - 3)
    operands = (
        by_tile(state),
        by_tile(rhs),
        by_tile(dinv),
        by_tile(lower_jac),
        by_tile(upper_jac),
        owner.reshape(1, fringe),
        donor_block.reshape(1, fringe),
        offsets,
        weights,
        receptor_perm,
    )
    made = pl.pallas_call(
        functools.partial(kernel, dims),
        out_shape=jax.ShapeDtypeStruct((width * rows, LANES), f32),
        in_specs=[pl.BlockSpec(memory_space=pltpu.HBM)] * 10,
        out_specs=vmem,
        scratch_shapes=[
            *(pltpu.VMEM(a.shape, a.dtype) for a in operands[:-1]),
            pltpu.SMEM(receptor_perm.shape, receptor_perm.dtype),
            dma((len(operands),)),
            pltpu.VMEM((nc, nz, ny, nx, width * rows, LANES), f32),
            pltpu.VMEM((slabs * crosses * rows, fringe), jnp.bfloat16),
            pltpu.VMEM((LANES, fringe), f32),
            pltpu.VMEM((width, fringe // LANES, LANES), f32),
            pltpu.VMEM((tiles * MAT_ROWS, LANES), f32),
            pltpu.VMEM((width * width, tiles, LANES), f32),
            pltpu.VMEM((tiles * VEC_ROWS, LANES), f32),
            pltpu.VMEM((slabs, MAT_ROWS, LANES), f32),
            pltpu.VMEM((slabs, VEC_ROWS, LANES), f32),
            pltpu.VMEM((slabs, VEC_ROWS, LANES), f32),
            pltpu.VMEM((tiles * VEC_ROWS, LANES), f32),
            dma((copies,)),
            dma((copies,)),
            dma((solvers,)),
            dma((slabs,)),
            dma((solvers,)),
            dma((slabs,)),
            dma((slabs,)),
            dma((solvers,)),
        ],
        compiler_params=pltpu.CompilerParams(
            collective_id=0, has_side_effects=True, vmem_limit_bytes=62 * 2**20
        ),
    )(*operands)
    made = jnp.swapaxes(made.reshape(width, tiles, planes, LANES), 1, 2)
    return made.reshape(width, planes, cells)


def solution(mesh):
    whole = ("slab", "cross")
    return jax.shard_map(
        body,
        mesh=mesh,
        in_specs=(
            P(None, "slab", "cross"),
            P(None, "slab", "cross"),
            P(None, None, "slab", "cross"),
            P(None, None, "slab", "cross"),
            P(None, None, "slab", "cross"),
            P(whole, None),
            P(whole),
            P(None, whole),
            P(None, whole),
            P(whole, None),
        ),
        out_specs=P(None, "slab", "cross"),
        check_vma=False,
    )
```
